128 devices in a mesh: zone: 16 (over y, x), subzone: 8 (over z, core).
Axes of the slice: x: 4, y: 4, z: 4, core: 2. Of those that a mesh axis runs over, the one named last changes fastest.
Arguments:
- spectra: bfloat16 [32768, 2, 16, 512], P(('zone', 'subzone')), may hold values from -6 to 6
- pair_first: int32 [16384], P(('zone', 'subzone')), may hold values from 0 to 32767, as said below
- pair_second: int32 [16384], P(('zone', 'subzone')), may hold values from 0 to 32767, as said below
- pair_valid: int32 [16384], P(('zone', 'subzone')), may hold values 0 or 1
Outputs:
- pair_peak: float32 [16384], P(('zone', 'subzone'))
- coherence: float32 [32768], P(('zone', 'subzone'))
The draws below stay inside these ranges and needn't reach their ends.
Inputs may be any that keep to these rules, and one draw needn't show every extreme that they name: `pair_first`: the pairs of block d (positions d * 128 onward, 128 of them) name as first sensor a sensor of block d (sensors d * 256 onward). `pair_second`: position q within block d names as second sensor a sensor of block (q), never the pair's first sensor.
All inputs are finite; a program needn't handle non-finite values. No bound on the sum of `pair_valid` on one device may be relied on, other than what follows from the above.
Results may differ from the reference program's by a relative error of at most 0.0028.
Values may be sent and summed in bfloat16 or wider, within the bound.
A program may use at most 128 MiB of HBM per device.

```python
import math
import jax
import jax.numpy as jnp
from jax import lax

SEG = 16
BINS = 512
LAGS = 512
S_DEV = 256
CAP = 1
OWNERS = 128
SENSORS = 32768
PAIRS = 16384


def pair_draw(key):
    inner = jax.random.fold_in(key, 7)
    key_first, key_second = jax.random.split(inner)
    position = jnp.arange(PAIRS, dtype=jnp.int32)
    owner = position // (CAP * OWNERS)
    target = position // CAP % OWNERS
    first_local = jax.random.randint(key_first, (PAIRS,), 0, S_DEV, dtype=jnp.int32)
    second_raw = jax.random.randint(key_second, (PAIRS,), 0, S_DEV - 1, dtype=jnp.int32)
    second_local = jnp.where((target == owner) & (second_raw >= first_local), second_raw + 1, second_raw)
    return (owner * S_DEV + first_local, target * S_DEV + second_local)


def draw_pair_first(key, part):
    return pair_draw(key)[0]


def draw_pair_second(key, part):
    return pair_draw(key)[1]


def plant(drawn, key, smallest, largest):
    index_at = [jax.random.randint(jax.random.fold_in(key, axis), (), 0, length) for axis, length in enumerate(drawn.shape)]
    main_axis = drawn.shape.index(max(drawn.shape))
    next_to = index_at[:main_axis] + [(index_at[main_axis] + 1) % drawn.shape[main_axis]] + index_at[main_axis + 1:]
    return drawn.at[tuple(index_at)].set(smallest).at[tuple(next_to)].set(largest)


def steps_of(rng, dims, shards, low, largest):
    gain = 1.0
    for dim, blocks in shards:
        steps = jax.random.uniform(jax.random.fold_in(jax.random.fold_in(rng, 6), dim), (blocks,), jnp.float32, low / len(shards), largest / len(shards))
        gain = gain * jnp.repeat(jnp.exp(steps), dims[dim] // blocks).reshape((-1,) + (1,) * (len(dims) - 1 - dim))
    return gain


def bell_draw(own_key, dims, deviation, reach, cuts=(), kind=jnp.bfloat16):
    result = deviation * jax.random.normal(own_key, dims, jnp.float32)
    if cuts:
        result = result * steps_of(own_key, dims, cuts, -0.22, 0.18)
    return jnp.clip(result, -reach, reach).astype(kind)


def setup_inputs(seed: int = 0) -> dict:
    key_of = jax.random.split(jax.random.key(seed), 5)
    return {
        "spectra": bell_draw(key_of[0], (SENSORS, 2, SEG, BINS), 1.0, 6.0, ((0, 128),)),
        "pair_first": draw_pair_first(jax.random.fold_in(key_of[4], 71), 0),
        "pair_second": draw_pair_second(jax.random.fold_in(key_of[4], 71), 0),
        "pair_valid": plant((jax.random.randint(key_of[3], (PAIRS,), 0, 4) < 3).astype(jnp.int32), jax.random.fold_in(key_of[3], 1), 0, 1),
    }


def lag_table(bins, lags):
    bin_index = jnp.arange(bins, dtype=jnp.int32)[:, None]
    lag_index = jnp.arange(lags, dtype=jnp.int32)[None, :] - lags // 2
    phase = jnp.mod(bin_index * lag_index, 2 * bins).astype(jnp.float32) * (math.pi / bins)
    return jnp.concatenate([jnp.cos(phase), -jnp.sin(phase)], 0).astype(jnp.bfloat16)

def tile_peaks(first_spec, second_spec, table):
    first_re = first_spec[:, 0].astype(jnp.float32)
    first_im = first_spec[:, 1].astype(jnp.float32)
    second_re = second_spec[:, 0].astype(jnp.float32)
    second_im = second_spec[:, 1].astype(jnp.float32)
    cross_re = first_re * second_re + first_im * second_im
    cross_im = first_im * second_re - first_re * second_im
    divisor = jnp.maximum(jnp.sqrt(cross_re * cross_re + cross_im * cross_im), 1.0)
    whitened = jnp.concatenate([cross_re / divisor, cross_im / divisor], -1).astype(jnp.bfloat16)
    correlation = jnp.einsum('psk,kl->psl', whitened.astype(jnp.float32), table.astype(jnp.float32), precision=lax.Precision.HIGHEST)
    bins = first_spec.shape[-1]
    averaged = lax.optimization_barrier(jnp.sum(correlation, axis=1)) * (bins ** (-0.5) / first_spec.shape[2])
    return lax.optimization_barrier(jnp.max(averaged, axis=-1))

def reference(spectra, pair_first, pair_second, pair_valid):
    table = lag_table(BINS, LAGS)

    def run_tile(items):
        first_spec = jnp.take(spectra, items[0], axis=0)
        second_spec = jnp.take(spectra, items[1], axis=0)
        return tile_peaks(first_spec, second_spec, table)
    peaks = lax.map(run_tile, (pair_first.reshape(-1, 128), pair_second.reshape(-1, 128))).reshape(-1)
    values = peaks * pair_valid.astype(jnp.float32)
    coherence = jnp.zeros((SENSORS,), jnp.float32).at[pair_first].add(values).at[pair_second].add(values)
    return (values, coherence)
```

```python
import itertools
import math

import jax
import jax.numpy as jnp
import numpy as np
from jax import lax
from jax.experimental import pallas as pl
from jax.experimental.pallas import tpu as pltpu
from jax.sharding import PartitionSpec as P

LAGS = 512
MESH = pl.DeviceIdType.MESH
SIDES = (4, 4, 4, 2)
STRIDES = (32, 8, 2, 1)
GROUP = 8


def lag_table(bins, lags):
    phase = np.mod(np.arange(bins)[:, None] * (np.arange(lags)[None, :] - lags // 2), 2 * bins)
    phase = phase.astype(np.float64) * (math.pi / bins)
    table = np.concatenate([np.cos(phase), -np.sin(phase)], 0)
    return jnp.asarray(table.astype(np.float32), dtype=jnp.bfloat16)


def offsets():
    seen, orbits = set(), []
    for chip in itertools.product(range(4), repeat=3):
        orbit = []
        for turn in range(3):
            turned = chip[turn:] + chip[:turn]
            for way in (turned, tuple(-a % 4 for a in turned)):
                if way not in seen:
                    seen.add(way)
                    orbit.append(way)
        if orbit:
            orbits.append(orbit)
    hops = lambda orbit: sum(min(a, 4 - a) for a in orbit[0])
    orbits.sort(key=lambda orbit: -hops(orbit))
    order = [chip + (core,) for orbit in orbits for core in range(2) for chip in orbit]
    order.remove((0, 0, 0, 0))
    return [(0, 0, 0, 0)] + order


def place(block):
    return (block // 8, block % 8)


def kernel(
    spectra_hbm, first_ref, second_ref, valid_ref, table_hbm, peak_out, coherence_out,
    spectra, table, outgoing, arrived, whitened, codes_out, codes_in, codes, peaks, returned,
    own_rows, target, source,
    load_sem, send_sem, code_send_sem, peak_send_sem, recv_sem, code_sem, code_copy_sem, peak_sem,
):
    zone, subzone = lax.axis_index("zone"), lax.axis_index("subzone")
    me = zone * 8 + subzone
    sensors = spectra.shape[0]
    count = arrived.shape[0]
    groups = count // GROUP
    order = offsets()

    loads = [
        pltpu.make_async_copy(spectra_hbm, spectra, load_sem.at[0]),
        pltpu.make_async_copy(table_hbm, table, load_sem.at[1]),
    ]
    for load in loads:
        load.start()

    here = (zone // 4, zone % 4, subzone // 2, subzone % 2)
    ahead = [[(h + o) % n * s for o in range(n)] for h, n, s in zip(here, SIDES, STRIDES)]
    for k, offset in enumerate(order):
        target[k] = sum(ahead[a][o] for a, o in enumerate(offset))
        source[k] = sum(ahead[a][-o % SIDES[a]] for a, o in enumerate(offset))

    barrier = pltpu.get_barrier_semaphore()

    @pl.loop(1, count)
    def _(k):
        pl.semaphore_signal(barrier, inc=1, device_id=place(target[k]), device_id_type=MESH)

    @pl.loop(0, count)
    def _(k):
        pair = target[k]
        in_use = valid_ref[pair]
        row = pl.ds(k, 1)
        codes_out[row] = jnp.full((1, 128), second_ref[pair] % sensors + in_use * sensors, jnp.int32)
        own_rows[0, row] = jnp.full((1, 128), first_ref[pair] % sensors + (1 - in_use) * sensors, jnp.int32)
        own_rows[1, row] = jnp.full((1, 128), pair + (1 - in_use) * sensors, jnp.int32)

    pl.semaphore_wait(barrier, count - 1)

    def code_copy(k):
        return pltpu.make_async_remote_copy(
            src_ref=codes_out.at[pl.ds(k, 1)],
            dst_ref=codes_in.at[pl.ds(k, 1)],
            send_sem=code_send_sem,
            recv_sem=code_sem,
            device_id=place(target[k]),
            device_id_type=MESH,
        )

    def spectrum_copy(k):
        return pltpu.make_async_remote_copy(
            src_ref=outgoing.at[k],
            dst_ref=arrived.at[k],
            send_sem=send_sem,
            recv_sem=recv_sem.at[k // GROUP],
            device_id=place(target[k]),
            device_id_type=MESH,
        )

    def peak_copy(k):
        return pltpu.make_async_remote_copy(
            src_ref=peaks.at[pl.ds(k, 1)],
            dst_ref=returned.at[pl.ds(k, 1)],
            send_sem=peak_send_sem,
            recv_sem=peak_sem,
            device_id=place(source[k]),
            device_id_type=MESH,
        )

    @pl.loop(1, count)
    def _(k):
        code_copy(k).start()

    own_code = pltpu.make_async_copy(codes_out.at[pl.ds(0, 1)], codes_in.at[pl.ds(0, 1)], code_sem)
    own_code.start()
    loads[0].wait()
    outgoing[0] = spectra[first_ref[me] % sensors]
    own_spectrum = pltpu.make_async_copy(outgoing.at[0], arrived.at[0], recv_sem.at[0])
    own_spectrum.start()

    @pl.loop(1, count)
    def _(k):
        outgoing[k] = spectra[first_ref[target[k]] % sensors]
        spectrum_copy(k).start()

    pltpu.make_async_copy(codes_in, codes_in, code_sem).wait()
    copy = pltpu.make_async_copy(codes_in, codes, code_copy_sem)
    copy.start()
    copy.wait()
    loads[1].wait()

    segments, bins = spectra.shape[2:]
    depth = GROUP * segments
    row_of = lax.broadcasted_iota(jnp.int32, (GROUP, depth), 0)
    segment_of = lax.broadcasted_iota(jnp.int32, (GROUP, depth), 1)
    adder = jnp.where(segment_of // segments == row_of, 1.0, 0.0).astype(jnp.bfloat16)
    scale = bins ** (-0.5) / segments

    @pl.loop(0, groups)
    def _(g):
        here = pl.ds(g * GROUP, GROUP)
        pltpu.make_async_copy(arrived.at[here], arrived.at[here], recv_sem.at[g]).wait()
        for i in range(GROUP):
            k = g * GROUP + i
            b = codes[k, 0] % sensors
            first_re = arrived[k, 0].astype(jnp.float32)
            first_im = arrived[k, 1].astype(jnp.float32)
            second_re = spectra[b, 0].astype(jnp.float32)
            second_im = spectra[b, 1].astype(jnp.float32)
            cross_re = first_re * second_re + first_im * second_im
            cross_im = first_im * second_re - first_re * second_im
            factor = lax.rsqrt(jnp.maximum(cross_re * cross_re + cross_im * cross_im, 1.0))
            rows = pl.ds(i * segments, segments)
            whitened[rows, 0:bins] = (cross_re * factor).astype(jnp.bfloat16)
            whitened[rows, bins:] = (cross_im * factor).astype(jnp.bfloat16)
        summed = jnp.dot(adder, whitened[...], preferred_element_type=jnp.float32)
        high = summed.astype(jnp.bfloat16)
        low = (summed - high.astype(jnp.float32)).astype(jnp.bfloat16)
        both = jnp.dot(jnp.concatenate([high, low], 0), table[...], preferred_element_type=jnp.float32)
        correlation = (both[:GROUP] + both[GROUP:]) * scale
        peaks[here] = jnp.broadcast_to(jnp.max(correlation, axis=-1, keepdims=True), (GROUP, 128))

        @pl.loop(jnp.where(g == 0, 1, 0), GROUP)
        def _(i):
            peak_copy(g * GROUP + i).start()

    own_peak = pltpu.make_async_copy(peaks.at[pl.ds(0, 1)], returned.at[pl.ds(0, 1)], peak_sem)
    own_peak.start()

    lane = lax.broadcasted_iota(jnp.int32, (count, 128), 1)

    def pick(rows, first, values):
        return jnp.sum(jnp.where(rows == lane + first, values, 0.0), axis=0, keepdims=True)

    seconds = [pick(codes_in[...], sensors + first, peaks[...]) for first in range(0, sensors, 128)]
    pltpu.make_async_copy(returned, returned, peak_sem).wait()
    values = returned[...]
    for i, first in enumerate(range(0, sensors, 128)):
        coherence_out[:, pl.ds(first, 128)] = seconds[i] + pick(own_rows[0], first, values)
    peak_out[...] = pick(own_rows[1], 0, values)

    @pl.loop(1, count)
    def _(k):
        code_copy(k).wait_send()
        spectrum_copy(k).wait_send()
        peak_copy(k).wait_send()


def on_device(spectra, pair_first, pair_second, pair_valid):
    sensors, trailing = spectra.shape[0], spectra.shape[1:]
    count = pair_first.shape[0]
    segments, bins = trailing[1:]
    any_space, smem, vmem = pl.ANY, pltpu.SMEM, pltpu.VMEM
    peak, coherence = pl.pallas_call(
        kernel,
        out_shape=(
            jax.ShapeDtypeStruct((1, count), jnp.float32),
            jax.ShapeDtypeStruct((1, sensors), jnp.float32),
        ),
        in_specs=[
            pl.BlockSpec(memory_space=any_space),
            pl.BlockSpec(memory_space=smem),
            pl.BlockSpec(memory_space=smem),
            pl.BlockSpec(memory_space=smem),
            pl.BlockSpec(memory_space=any_space),
        ],
        out_specs=[pl.BlockSpec(memory_space=vmem)] * 2,
        scratch_shapes=[
            vmem((sensors,) + trailing, jnp.bfloat16),
            vmem((2 * bins, LAGS), jnp.bfloat16),
            vmem((count,) + trailing, jnp.bfloat16),
            vmem((count,) + trailing, jnp.bfloat16),
            vmem((GROUP * segments, 2 * bins), jnp.bfloat16),
            vmem((count, 128), jnp.int32),
            vmem((count, 128), jnp.int32),
            smem((count, 128), jnp.int32),
            vmem((count, 128), jnp.float32),
            vmem((count, 128), jnp.float32),
            vmem((2, count, 128), jnp.int32),
            smem((count,), jnp.int32),
            smem((count,), jnp.int32),
            pltpu.SemaphoreType.DMA((2,)),
            pltpu.SemaphoreType.DMA,
            pltpu.SemaphoreType.DMA,
            pltpu.SemaphoreType.DMA,
            pltpu.SemaphoreType.DMA((count // GROUP,)),
            pltpu.SemaphoreType.DMA,
            pltpu.SemaphoreType.DMA,
            pltpu.SemaphoreType.DMA,
        ],
        compiler_params=pltpu.CompilerParams(
            collective_id=1, has_side_effects=True, vmem_limit_bytes=40 << 20
        ),
    )(spectra, pair_first, pair_second, pair_valid, lag_table(bins, LAGS))
    return (peak.reshape(-1), coherence.reshape(-1))


def solution(mesh):
    blocks = ("zone", "subzone")
    return jax.shard_map(
        on_device,
        mesh=mesh,
        in_specs=(P(blocks, None, None, None), P(blocks), P(blocks), P(blocks)),
        out_specs=(P(blocks), P(blocks)),
        check_vma=False,
    )
```

```python
import itertools
import math

import jax
import jax.numpy as jnp
import numpy as np
from jax import lax
from jax.experimental import pallas as pl
from jax.experimental.pallas import tpu as pltpu
from jax.sharding import PartitionSpec as P

LAGS = 512
MESH = pl.DeviceIdType.MESH
SIDES = (4, 4, 4, 2)
STRIDES = (32, 8, 2, 1)
GROUP = 8


def lag_table(bins, lags):
    phase = np.mod(np.arange(bins)[:, None] * (np.arange(lags)[None, :] - lags // 2), 2 * bins)
    phase = phase.astype(np.float64) * (math.pi / bins)
    table = np.concatenate([np.cos(phase), -np.sin(phase)], 0)
    return jnp.asarray(table.astype(np.float32), dtype=jnp.bfloat16)


def orbit(chip):
    found = []
    for turn in range(3):
        turned = chip[turn:] + chip[:turn]
        for way in (turned, tuple(-a % 4 for a in turned)):
            if way not in found:
                found.append(way)
    return found


IN_LINE = [((2, 0, 0), (0, 1))]
IN_PLANE = [((2, 2, 0), (0, 1))]
OTHERS = [
    (chip, (0, 1))
    for chip in (
        (2, 2, 2), (1, 2, 2), (1, 1, 2), (1, 3, 2), (1, 1, 3), (1, 1, 1),
        (1, 2, 0), (2, 1, 0), (1, 3, 0), (1, 1, 0), (1, 0, 0),
    )
]


def spread(parts):
    return [way + (core,) for chip, cores in parts for core in cores for way in orbit(chip)]


def offsets():
    first = [(0, 0, 0, 0), (0, 0, 0, 1)] + spread(IN_LINE)
    second = first + spread(IN_PLANE)
    order = second + spread(OTHERS)
    assert len(set(order)) == len(order) == 128
    return order, len(first), len(second)


def place(block):
    return (block // 8, block % 8)


def kernel(
    spectra_hbm, first_hbm, second_hbm, valid_hbm, table_hbm, peak_out, coherence_out,
    spectra, table, outgoing, arrived, whitened, codes_out, codes_in, codes, peaks, returned,
    own_rows, first_ref, second_ref, valid_ref, target, source,
    load_sem, send_sem, code_send_sem, peak_send_sem, recv_sem, code_sem, code_copy_sem, peak_sem, plane_sem, cube_sem,
):
    zone, subzone = lax.axis_index("zone"), lax.axis_index("subzone")
    me = zone * 8 + subzone
    sensors = spectra.shape[0]
    count = arrived.shape[0]
    groups = count // GROUP
    order, lines, planes = offsets()

    loads = [
        pltpu.make_async_copy(a, b, load_sem.at[i])
        for i, (a, b) in enumerate(
            [(first_hbm, first_ref), (second_hbm, second_ref), (valid_hbm, valid_ref), (spectra_hbm, spectra), (table_hbm, table)]
        )
    ]
    for load in loads:
        load.start()

    here = (zone // 4, zone % 4, subzone // 2, subzone % 2)
    ahead = [[(h + o) % n * s for o in range(n)] for h, n, s in zip(here, SIDES, STRIDES)]

    def signal(semaphore, ways):
        for way in ways:
            other = sum(ahead[a][o] for a, o in enumerate(way))
            pl.semaphore_signal(semaphore, inc=1, device_id=place(other), device_id_type=MESH)

    along_y = [(i, 0, 0, 0) for i in (1, 3, 2)]
    along_x = [(0, i, 0, 0) for i in (1, 3, 2)]
    barrier = pltpu.get_barrier_semaphore()
    in_line = [
        way[:3] + (core,) for i in (2, 1, 3) for way in ((i, 0, 0), (0, i, 0), (0, 0, i)) for core in range(2)
    ] + [(0, 0, 0, 1)]
    signal(barrier, in_line)

    for k, offset in enumerate(order):
        target[k] = sum(ahead[a][o] for a, o in enumerate(offset))
        source[k] = sum(ahead[a][-o % SIDES[a]] for a, o in enumerate(offset))
    for load in loads[:3]:
        load.wait()

    @pl.loop(0, count)
    def _(k):
        pair = target[k]
        in_use = valid_ref[pair]
        row = pl.ds(k, 1)
        codes_out[row] = jnp.full((1, 128), second_ref[pair] % sensors + in_use * sensors, jnp.int32)
        own_rows[0, row] = jnp.full((1, 128), first_ref[pair] % sensors + (1 - in_use) * sensors, jnp.int32)
        own_rows[1, row] = jnp.full((1, 128), pair + (1 - in_use) * sensors, jnp.int32)

    loads[3].wait()

    def code_copy(k):
        return pltpu.make_async_remote_copy(
            src_ref=codes_out.at[pl.ds(k, 1)],
            dst_ref=codes_in.at[pl.ds(k, 1)],
            send_sem=code_send_sem,
            recv_sem=code_sem,
            device_id=place(target[k]),
            device_id_type=MESH,
        )

    def spectrum_copy(k):
        return pltpu.make_async_remote_copy(
            src_ref=outgoing.at[k],
            dst_ref=arrived.at[k],
            send_sem=send_sem,
            recv_sem=recv_sem.at[k // GROUP],
            device_id=place(target[k]),
            device_id_type=MESH,
        )

    def peak_copy(k):
        return pltpu.make_async_remote_copy(
            src_ref=peaks.at[pl.ds(k, 1)],
            dst_ref=returned.at[pl.ds(k, 1)],
            send_sem=peak_send_sem,
            recv_sem=peak_sem,
            device_id=place(source[k]),
            device_id_type=MESH,
        )

    def send(low, high):
        @pl.loop(low, high)
        def _(k):
            outgoing[k] = spectra[first_ref[target[k]] % sensors]
            spectrum_copy(k).start()

    own_code = pltpu.make_async_copy(codes_out.at[pl.ds(0, 1)], codes_in.at[pl.ds(0, 1)], code_sem)
    own_code.start()
    outgoing[0] = spectra[first_ref[me] % sensors]
    own_spectrum = pltpu.make_async_copy(outgoing.at[0], arrived.at[0], recv_sem.at[0])
    own_spectrum.start()
    pl.semaphore_wait(barrier, len(in_line))
    signal(plane_sem, along_x + along_y)
    send(1, lines)
    pl.semaphore_wait(plane_sem, 6)
    signal(cube_sem, along_x)
    send(lines, planes)
    pl.semaphore_wait(cube_sem, 3)

    @pl.loop(1, count)
    def _(k):
        code_copy(k).start()

    send(planes, count)

    pltpu.make_async_copy(codes_in, codes_in, code_sem).wait()
    copy = pltpu.make_async_copy(codes_in, codes, code_copy_sem)
    copy.start()
    copy.wait()
    loads[4].wait()

    segments, bins = spectra.shape[2:]
    depth = GROUP * segments
    row_of = lax.broadcasted_iota(jnp.int32, (GROUP, depth), 0)
    segment_of = lax.broadcasted_iota(jnp.int32, (GROUP, depth), 1)
    adder = jnp.where(segment_of // segments == row_of, 1.0, 0.0).astype(jnp.bfloat16)
    scale = bins ** (-0.5) / segments

    @pl.loop(0, groups)
    def _(g):
        here = pl.ds(g * GROUP, GROUP)
        pltpu.make_async_copy(arrived.at[here], arrived.at[here], recv_sem.at[g]).wait()
        for i in range(GROUP):
            k = g * GROUP + i
            b = codes[k, 0] % sensors
            first_re = arrived[k, 0].astype(jnp.float32)
            first_im = arrived[k, 1].astype(jnp.float32)
            second_re = spectra[b, 0].astype(jnp.float32)
            second_im = spectra[b, 1].astype(jnp.float32)
            cross_re = first_re * second_re + first_im * second_im
            cross_im = first_im * second_re - first_re * second_im
            factor = lax.rsqrt(jnp.maximum(cross_re * cross_re + cross_im * cross_im, 1.0))
            rows = pl.ds(i * segments, segments)
            whitened[rows, 0:bins] = (cross_re * factor).astype(jnp.bfloat16)
            whitened[rows, bins:] = (cross_im * factor).astype(jnp.bfloat16)
        summed = jnp.dot(adder, whitened[...], preferred_element_type=jnp.float32)
        high = summed.astype(jnp.bfloat16)
        low = (summed - high.astype(jnp.float32)).astype(jnp.bfloat16)
        both = jnp.dot(jnp.concatenate([high, low], 0), table[...], preferred_element_type=jnp.float32)
        correlation = (both[:GROUP] + both[GROUP:]) * scale
        peaks[here] = jnp.broadcast_to(jnp.max(correlation, axis=-1, keepdims=True), (GROUP, 128))

        @pl.loop(jnp.where(g == 0, 1, 0), GROUP)
        def _(i):
            peak_copy(g * GROUP + i).start()

    own_peak = pltpu.make_async_copy(peaks.at[pl.ds(0, 1)], returned.at[pl.ds(0, 1)], peak_sem)
    own_peak.start()

    lane = lax.broadcasted_iota(jnp.int32, (count, 128), 1)

    def pick(rows, first, values):
        return jnp.sum(jnp.where(rows == lane + first, values, 0.0), axis=0, keepdims=True)

    seconds = [pick(codes_in[...], sensors + first, peaks[...]) for first in range(0, sensors, 128)]
    sent = pl.ds(1, count - 1)
    for buffer, semaphore in ((codes_out, code_send_sem), (outgoing, send_sem), (peaks, peak_send_sem)):
        pltpu.make_async_copy(buffer.at[sent], buffer.at[sent], semaphore).wait()
    pltpu.make_async_copy(returned, returned, peak_sem).wait()
    values = returned[...]
    for i, first in enumerate(range(0, sensors, 128)):
        coherence_out[:, pl.ds(first, 128)] = seconds[i] + pick(own_rows[0], first, values)
    peak_out[...] = pick(own_rows[1], 0, values)


def on_device(spectra, pair_first, pair_second, pair_valid):
    sensors, trailing = spectra.shape[0], spectra.shape[1:]
    count = pair_first.shape[0]
    segments, bins = trailing[1:]
    hbm, smem, vmem = pltpu.HBM, pltpu.SMEM, pltpu.VMEM
    peak, coherence = pl.pallas_call(
        kernel,
        out_shape=(
            jax.ShapeDtypeStruct((1, count), jnp.float32),
            jax.ShapeDtypeStruct((1, sensors), jnp.float32),
        ),
        in_specs=[pl.BlockSpec(memory_space=hbm)] * 5,
        out_specs=[pl.BlockSpec(memory_space=vmem)] * 2,
        scratch_shapes=[
            vmem((sensors,) + trailing, jnp.bfloat16),
            vmem((2 * bins, LAGS), jnp.bfloat16),
            vmem((count,) + trailing, jnp.bfloat16),
            vmem((count,) + trailing, jnp.bfloat16),
            vmem((GROUP * segments, 2 * bins), jnp.bfloat16),
            vmem((count, 128), jnp.int32),
            vmem((count, 128), jnp.int32),
            smem((count, 128), jnp.int32),
            vmem((count, 128), jnp.float32),
            vmem((count, 128), jnp.float32),
            vmem((2, count, 128), jnp.int32),
            smem((count,), jnp.int32),
            smem((count,), jnp.int32),
            smem((count,), jnp.int32),
            smem((count,), jnp.int32),
            smem((count,), jnp.int32),
            pltpu.SemaphoreType.DMA((5,)),
            pltpu.SemaphoreType.DMA,
            pltpu.SemaphoreType.DMA,
            pltpu.SemaphoreType.DMA,
            pltpu.SemaphoreType.DMA((count // GROUP,)),
            pltpu.SemaphoreType.DMA,
            pltpu.SemaphoreType.DMA,
            pltpu.SemaphoreType.DMA,
            pltpu.SemaphoreType.REGULAR,
            pltpu.SemaphoreType.REGULAR,
        ],
        compiler_params=pltpu.CompilerParams(
            collective_id=1, has_side_effects=True, vmem_limit_bytes=60 << 20
        ),
    )(spectra, pair_first, pair_second, pair_valid, lag_table(bins, LAGS))
    return (peak.reshape(-1), coherence.reshape(-1))


def solution(mesh):
    blocks = ("zone", "subzone")
    return jax.shard_map(
        on_device,
        mesh=mesh,
        in_specs=(P(blocks, None, None, None), P(blocks), P(blocks), P(blocks)),
        out_specs=(P(blocks), P(blocks)),
        check_vma=False,
    )
```

```python
import itertools
import math

import jax
import jax.numpy as jnp
import numpy as np
from jax import lax
from jax.experimental import pallas as pl
from jax.experimental.pallas import tpu as pltpu
from jax.sharding import PartitionSpec as P

LAGS = 512
MESH = pl.DeviceIdType.MESH
SIDES = (4, 4, 4, 2)
STRIDES = (32, 8, 2, 1)
GROUP = 8
CODES_AT = 16


def lag_table(bins, lags):
    phase = np.mod(np.arange(bins)[:, None] * (np.arange(lags)[None, :] - lags // 2), 2 * bins)
    phase = phase.astype(np.float64) * (math.pi / bins)
    table = np.concatenate([np.cos(phase), -np.sin(phase)], 0)
    return jnp.asarray(table.astype(np.float32), dtype=jnp.bfloat16)


def orbit(chip):
    found = []
    for turn in range(3):
        turned = chip[turn:] + chip[:turn]
        for way in (turned, tuple(-a % 4 for a in turned)):
            if way not in found:
                found.append(way)
    return found


IN_LINE = [((2, 0, 0), (0, 1))]
IN_PLANE = [((2, 2, 0), (0, 1))]
OTHERS = [
    (chip, (0, 1))
    for chip in (
        (2, 2, 2), (1, 2, 2), (1, 1, 2), (1, 3, 2), (1, 1, 3), (1, 1, 1),
        (1, 2, 0), (2, 1, 0), (1, 3, 0), (1, 1, 0), (1, 0, 0),
    )
]


def spread(parts):
    return [way + (core,) for chip, cores in parts for core in cores for way in orbit(chip)]


def offsets():
    first = [(0, 0, 0, 0), (0, 0, 0, 1)] + spread(IN_LINE)
    second = first + spread(IN_PLANE)
    order = second + spread(OTHERS)
    assert len(set(order)) == len(order) == 128
    return order, len(first), len(second)


def place(block):
    return (block // 8, block % 8)


def kernel(
    spectra_hbm, first_hbm, second_hbm, valid_hbm, table_hbm, peak_out, coherence_out,
    spectra, table, outgoing, arrived, whitened, codes_out, codes_in, code_row, codes, peaks, returned,
    own_rows, first_ref, second_ref, valid_ref, target, source,
    load_sem, send_sem, code_send_sem, peak_send_sem, recv_sem, code_sem, code_copy_sem, peak_sem, plane_sem, cube_sem,
):
    zone, subzone = lax.axis_index("zone"), lax.axis_index("subzone")
    me = zone * 8 + subzone
    sensors = spectra.shape[0]
    count = arrived.shape[0]
    groups = count // GROUP
    order, lines, planes = offsets()

    loads = [
        pltpu.make_async_copy(a, b, load_sem.at[i])
        for i, (a, b) in enumerate(
            [(first_hbm, first_ref), (second_hbm, second_ref), (valid_hbm, valid_ref), (table_hbm, table)]
        )
    ]
    share = sensors // 4
    parts = tuple(
        pltpu.make_async_copy(spectra_hbm.at[pl.ds(i * share, share)], spectra.at[pl.ds(i * share, share)], load_sem.at[4 + i])
        for i in range(4)
    )
    for load in (loads[0],) + parts + tuple(loads[1:]):
        load.start()

    here = (zone // 4, zone % 4, subzone // 2, subzone % 2)
    ahead = [[(h + o) % n * s for o in range(n)] for h, n, s in zip(here, SIDES, STRIDES)]

    def signal(semaphore, ways):
        for way in ways:
            other = sum(ahead[a][o] for a, o in enumerate(way))
            pl.semaphore_signal(semaphore, inc=1, device_id=place(other), device_id_type=MESH)

    along_y = [(i, 0, 0, 0) for i in (1, 3, 2)]
    along_x = [(0, i, 0, 0) for i in (1, 3, 2)]
    barrier = pltpu.get_barrier_semaphore()
    in_line = [
        way[:3] + (core,) for i in (2, 1, 3) for way in ((i, 0, 0), (0, i, 0), (0, 0, i)) for core in range(2)
    ] + [(0, 0, 0, 1)]
    signal(barrier, in_line)

    def locate(low, high):
        for k in range(low, high):
            target[k] = sum(ahead[a][o] for a, o in enumerate(order[k]))

    pl.semaphore_wait(barrier, len(in_line))
    signal(plane_sem, along_x + along_y)
    locate(0, planes)
    for load in (loads[0],) + parts:
        load.wait()

    def code_copy(k):
        return pltpu.make_async_remote_copy(
            src_ref=codes_out.at[pl.ds(k, 1)],
            dst_ref=codes_in.at[pl.ds(k, 1)],
            send_sem=code_send_sem,
            recv_sem=code_sem,
            device_id=place(target[k]),
            device_id_type=MESH,
        )

    def spectrum_copy(k):
        return pltpu.make_async_remote_copy(
            src_ref=outgoing.at[k],
            dst_ref=arrived.at[k],
            send_sem=send_sem,
            recv_sem=recv_sem.at[k // GROUP],
            device_id=place(target[k]),
            device_id_type=MESH,
        )

    def peak_copy(k):
        return pltpu.make_async_remote_copy(
            src_ref=peaks.at[pl.ds(k, 1)],
            dst_ref=returned.at[pl.ds(k, 1)],
            send_sem=peak_send_sem,
            recv_sem=peak_sem,
            device_id=place(source[k]),
            device_id_type=MESH,
        )

    def pack(k):
        outgoing[k] = spectra[first_ref[target[k]] % sensors]

    def send(low, high):
        @pl.loop(low, high)
        def _(k):
            pack(k)
            spectrum_copy(k).start()

    send(1, lines)
    pl.semaphore_wait(plane_sem, 6)
    signal(cube_sem, along_x)
    send(lines, planes)
    locate(planes, count)
    pl.semaphore_wait(cube_sem, 3)
    send(planes, CODES_AT)
    for load in loads[1:3]:
        load.wait()
    for k, offset in enumerate(order):
        source[k] = sum(ahead[a][-o % SIDES[a]] for a, o in enumerate(offset))

    @pl.loop(0, count)
    def _(k):
        pair = target[k]
        in_use = valid_ref[pair]
        row = pl.ds(k, 1)
        codes_out[row] = jnp.full((1, 128), second_ref[pair] % sensors + in_use * sensors, jnp.int32)
        own_rows[0, row] = jnp.full((1, 128), first_ref[pair] % sensors + (1 - in_use) * sensors, jnp.int32)
        own_rows[1, row] = jnp.full((1, 128), pair + (1 - in_use) * sensors, jnp.int32)

        @pl.when(k > 0)
        def _():
            code_copy(k).start()

    pack(0)
    own_spectrum = pltpu.make_async_copy(outgoing.at[0], arrived.at[0], recv_sem.at[0])
    own_spectrum.start()
    own_code = pltpu.make_async_copy(codes_out.at[pl.ds(0, 1)], codes_in.at[pl.ds(0, 1)], code_sem)
    own_code.start()
    send(CODES_AT, count)

    pltpu.make_async_copy(codes_in, codes_in, code_sem).wait()
    lane = lax.broadcasted_iota(jnp.int32, (count, 128), 1)
    slot = lax.broadcasted_iota(jnp.int32, (count, 128), 0)
    code_row[...] = jnp.sum(jnp.where(lane == slot, codes_in[...], 0), axis=0, keepdims=True)
    copy = pltpu.make_async_copy(code_row, codes, code_copy_sem)
    copy.start()
    copy.wait()
    loads[3].wait()

    segments, bins = spectra.shape[2:]
    depth = GROUP * segments
    row_of = lax.broadcasted_iota(jnp.int32, (GROUP, depth), 0)
    segment_of = lax.broadcasted_iota(jnp.int32, (GROUP, depth), 1)
    adder = jnp.where(segment_of // segments == row_of, 1.0, 0.0).astype(jnp.bfloat16)
    scale = bins ** (-0.5) / segments

    @pl.loop(0, groups)
    def _(g):
        here = pl.ds(g * GROUP, GROUP)
        pltpu.make_async_copy(arrived.at[here], arrived.at[here], recv_sem.at[g]).wait()
        for i in range(GROUP):
            k = g * GROUP + i
            b = codes[0, k] % sensors
            first_re = arrived[k, 0].astype(jnp.float32)
            first_im = arrived[k, 1].astype(jnp.float32)
            second_re = spectra[b, 0].astype(jnp.float32)
            second_im = spectra[b, 1].astype(jnp.float32)
            cross_re = first_re * second_re + first_im * second_im
            cross_im = first_im * second_re - first_re * second_im
            factor = lax.rsqrt(jnp.maximum(cross_re * cross_re + cross_im * cross_im, 1.0))
            rows = pl.ds(i * segments, segments)
            whitened[rows, 0:bins] = (cross_re * factor).astype(jnp.bfloat16)
            whitened[rows, bins:] = (cross_im * factor).astype(jnp.bfloat16)
        summed = jnp.dot(adder, whitened[...], preferred_element_type=jnp.float32)
        high = summed.astype(jnp.bfloat16)
        low = (summed - high.astype(jnp.float32)).astype(jnp.bfloat16)
        both = jnp.dot(jnp.concatenate([high, low], 0), table[...], preferred_element_type=jnp.float32)
        correlation = (both[:GROUP] + both[GROUP:]) * scale
        peaks[here] = jnp.broadcast_to(jnp.max(correlation, axis=-1, keepdims=True), (GROUP, 128))

        @pl.loop(jnp.where(g == 0, 1, 0), GROUP)
        def _(i):
            peak_copy(g * GROUP + i).start()

    own_peak = pltpu.make_async_copy(peaks.at[pl.ds(0, 1)], returned.at[pl.ds(0, 1)], peak_sem)
    own_peak.start()

    def pick(rows, first, values):
        return jnp.sum(jnp.where(rows == lane + first, values, 0.0), axis=0, keepdims=True)

    seconds = [pick(codes_in[...], sensors + first, peaks[...]) for first in range(0, sensors, 128)]
    sent = pl.ds(1, count - 1)
    for buffer, semaphore in ((codes_out, code_send_sem), (outgoing, send_sem), (peaks, peak_send_sem)):
        pltpu.make_async_copy(buffer.at[sent], buffer.at[sent], semaphore).wait()
    pltpu.make_async_copy(returned, returned, peak_sem).wait()
    values = returned[...]
    for i, first in enumerate(range(0, sensors, 128)):
        coherence_out[:, pl.ds(first, 128)] = seconds[i] + pick(own_rows[0], first, values)
    peak_out[...] = pick(own_rows[1], 0, values)


def on_device(spectra, pair_first, pair_second, pair_valid):
    sensors, trailing = spectra.shape[0], spectra.shape[1:]
    count = pair_first.shape[0]
    segments, bins = trailing[1:]
    hbm, smem, vmem = pltpu.HBM, pltpu.SMEM, pltpu.VMEM
    peak, coherence = pl.pallas_call(
        kernel,
        out_shape=(
            vmem((1, count), jnp.float32),
            vmem((1, sensors), jnp.float32),
        ),
        in_specs=[pl.BlockSpec(memory_space=hbm)] * 5,
        out_specs=[pl.BlockSpec(memory_space=vmem)] * 2,
        scratch_shapes=[
            vmem((sensors,) + trailing, jnp.bfloat16),
            vmem((2 * bins, LAGS), jnp.bfloat16),
            vmem((count,) + trailing, jnp.bfloat16),
            vmem((count,) + trailing, jnp.bfloat16),
            vmem((GROUP * segments, 2 * bins), jnp.bfloat16),
            vmem((count, 128), jnp.int32),
            vmem((count, 128), jnp.int32),
            vmem((1, count), jnp.int32),
            smem((1, count), jnp.int32),
            vmem((count, 128), jnp.float32),
            vmem((count, 128), jnp.float32),
            vmem((2, count, 128), jnp.int32),
            smem((count,), jnp.int32),
            smem((count,), jnp.int32),
            smem((count,), jnp.int32),
            smem((count,), jnp.int32),
            smem((count,), jnp.int32),
            pltpu.SemaphoreType.DMA((8,)),
            pltpu.SemaphoreType.DMA,
            pltpu.SemaphoreType.DMA,
            pltpu.SemaphoreType.DMA,
            pltpu.SemaphoreType.DMA((count // GROUP,)),
            pltpu.SemaphoreType.DMA,
            pltpu.SemaphoreType.DMA,
            pltpu.SemaphoreType.DMA,
            pltpu.SemaphoreType.REGULAR,
            pltpu.SemaphoreType.REGULAR,
        ],
        compiler_params=pltpu.CompilerParams(
            collective_id=1, has_side_effects=True, vmem_limit_bytes=60 << 20
        ),
    )(spectra, pair_first, pair_second, pair_valid, lag_table(bins, LAGS))
    return (peak.reshape(-1), coherence.reshape(-1))


def solution(mesh):
    blocks = ("zone", "subzone")
    return jax.shard_map(
        on_device,
        mesh=mesh,
        in_specs=(P(blocks, None, None, None), P(blocks), P(blocks), P(blocks)),
        out_specs=(P(blocks), P(blocks)),
        check_vma=False,
    )
```

```python
import itertools
import math

import jax
import jax.numpy as jnp
import numpy as np
from jax import lax
from jax.experimental import pallas as pl
from jax.experimental.pallas import tpu as pltpu
from jax.sharding import PartitionSpec as P

LAGS = 512
MESH = pl.DeviceIdType.MESH
SIDES = (4, 4, 4, 2)
STRIDES = (32, 8, 2, 1)
GROUP = 8
CODES_AT = 16


def lag_table(bins, lags):
    phase = np.mod(np.arange(bins)[:, None] * (np.arange(lags)[None, :] - lags // 2), 2 * bins)
    phase = phase.astype(np.float64) * (math.pi / bins)
    table = np.concatenate([np.cos(phase), -np.sin(phase)], 0)
    return jnp.asarray(table.astype(np.float32), dtype=jnp.bfloat16)


def orbit(chip):
    found = []
    for turn in range(3):
        turned = chip[turn:] + chip[:turn]
        for way in (turned, tuple(-a % 4 for a in turned)):
            if way not in found:
                found.append(way)
    return found


IN_LINE = [((2, 0, 0), (0, 1))]
IN_PLANE = [((2, 2, 0), (0, 1))]
OTHERS = [
    (chip, (0, 1))
    for chip in (
        (2, 2, 2), (1, 2, 2), (1, 1, 2), (1, 3, 2), (1, 1, 3), (1, 1, 1),
        (1, 2, 0), (2, 1, 0), (1, 3, 0), (1, 1, 0), (1, 0, 0),
    )
]


def spread(parts):
    return [
        way + ((i + core) % 2,) for chip, cores in parts for core in cores for i, way in enumerate(orbit(chip))
    ]


def offsets():
    first = [(0, 0, 0, 0), (0, 0, 0, 1)] + spread(IN_LINE)
    second = first + spread(IN_PLANE)
    order = second + spread(OTHERS)
    assert len(set(order)) == len(order) == 128
    return order, len(first), len(second)


def place(block):
    return (block // 8, block % 8)


def kernel(
    spectra_hbm, first_hbm, second_hbm, valid_hbm, table_hbm, peak_out, coherence_out,
    spectra, table, outgoing, arrived, whitened, codes_out, codes_in, code_row, codes, peaks, returned,
    own_rows, first_ref, second_ref, valid_ref, target, source,
    load_sem, send_sem, code_send_sem, peak_send_sem, recv_sem, code_sem, code_copy_sem, peak_sem, plane_sem, cube_sem,
):
    zone, subzone = lax.axis_index("zone"), lax.axis_index("subzone")
    me = zone * 8 + subzone
    sensors = spectra.shape[0]
    count = arrived.shape[0]
    groups = count // GROUP
    order, lines, planes = offsets()

    loads = [
        pltpu.make_async_copy(a, b, load_sem.at[i])
        for i, (a, b) in enumerate(
            [(first_hbm, first_ref), (second_hbm, second_ref), (valid_hbm, valid_ref), (table_hbm, table)]
        )
    ]
    share = sensors // 4
    parts = tuple(
        pltpu.make_async_copy(spectra_hbm.at[pl.ds(i * share, share)], spectra.at[pl.ds(i * share, share)], load_sem.at[4 + i])
        for i in range(4)
    )
    for load in (loads[0],) + parts + tuple(loads[1:]):
        load.start()

    here = (zone // 4, zone % 4, subzone // 2, subzone % 2)
    ahead = [[(h + o) % n * s for o in range(n)] for h, n, s in zip(here, SIDES, STRIDES)]

    def signal(semaphore, ways):
        for way in ways:
            other = sum(ahead[a][o] for a, o in enumerate(way))
            pl.semaphore_signal(semaphore, inc=1, device_id=place(other), device_id_type=MESH)

    along_y = [(i, 0, 0, 0) for i in (1, 3, 2)]
    along_x = [(0, i, 0, 0) for i in (1, 3, 2)]
    barrier = pltpu.get_barrier_semaphore()
    in_line = [
        way[:3] + (core,) for i in (2, 1, 3) for way in ((i, 0, 0), (0, i, 0), (0, 0, i)) for core in range(2)
    ] + [(0, 0, 0, 1)]
    signal(barrier, in_line)

    def locate(low, high):
        for k in range(low, high):
            target[k] = sum(ahead[a][o] for a, o in enumerate(order[k]))

    pl.semaphore_wait(barrier, len(in_line))
    signal(plane_sem, along_x + along_y)
    locate(0, planes)
    for load in (loads[0],) + parts:
        load.wait()

    def code_copy(k):
        return pltpu.make_async_remote_copy(
            src_ref=codes_out.at[pl.ds(k, 1)],
            dst_ref=codes_in.at[pl.ds(k, 1)],
            send_sem=code_send_sem,
            recv_sem=code_sem,
            device_id=place(target[k]),
            device_id_type=MESH,
        )

    def spectrum_copy(k):
        return pltpu.make_async_remote_copy(
            src_ref=outgoing.at[k],
            dst_ref=arrived.at[k],
            send_sem=send_sem,
            recv_sem=recv_sem.at[k // GROUP],
            device_id=place(target[k]),
            device_id_type=MESH,
        )

    def peak_copy(k):
        return pltpu.make_async_remote_copy(
            src_ref=peaks.at[pl.ds(k, 1)],
            dst_ref=returned.at[pl.ds(k, 1)],
            send_sem=peak_send_sem,
            recv_sem=peak_sem,
            device_id=place(source[k]),
            device_id_type=MESH,
        )

    def pack(k):
        outgoing[k] = spectra[first_ref[target[k]] % sensors]

    def send(low, high):
        @pl.loop(low, high)
        def _(k):
            pack(k)
            spectrum_copy(k).start()

    send(1, lines)
    pl.semaphore_wait(plane_sem, 6)
    signal(cube_sem, along_x)
    send(lines, planes)
    locate(planes, count)
    pl.semaphore_wait(cube_sem, 3)
    send(planes, CODES_AT)
    for load in loads[1:3]:
        load.wait()
    for k, offset in enumerate(order):
        source[k] = sum(ahead[a][-o % SIDES[a]] for a, o in enumerate(offset))

    @pl.loop(0, count)
    def _(k):
        pair = target[k]
        in_use = valid_ref[pair]
        row = pl.ds(k, 1)
        codes_out[row] = jnp.full((1, 128), second_ref[pair] % sensors + in_use * sensors, jnp.int32)
        own_rows[0, row] = jnp.full((1, 128), first_ref[pair] % sensors + (1 - in_use) * sensors, jnp.int32)
        own_rows[1, row] = jnp.full((1, 128), pair + (1 - in_use) * sensors, jnp.int32)

        @pl.when(k > 0)
        def _():
            code_copy(k).start()

    pack(0)
    own_spectrum = pltpu.make_async_copy(outgoing.at[0], arrived.at[0], recv_sem.at[0])
    own_spectrum.start()
    own_code = pltpu.make_async_copy(codes_out.at[pl.ds(0, 1)], codes_in.at[pl.ds(0, 1)], code_sem)
    own_code.start()
    send(CODES_AT, count)

    pltpu.make_async_copy(codes_in, codes_in, code_sem).wait()
    lane = lax.broadcasted_iota(jnp.int32, (count, 128), 1)
    slot = lax.broadcasted_iota(jnp.int32, (count, 128), 0)
    code_row[...] = jnp.sum(jnp.where(lane == slot, codes_in[...], 0), axis=0, keepdims=True)
    copy = pltpu.make_async_copy(code_row, codes, code_copy_sem)
    copy.start()
    copy.wait()
    loads[3].wait()

    segments, bins = spectra.shape[2:]
    depth = GROUP * segments
    row_of = lax.broadcasted_iota(jnp.int32, (GROUP, depth), 0)
    segment_of = lax.broadcasted_iota(jnp.int32, (GROUP, depth), 1)
    adder = jnp.where(segment_of // segments == row_of, 1.0, 0.0).astype(jnp.bfloat16)
    scale = bins ** (-0.5) / segments

    @pl.loop(0, groups)
    def _(g):
        here = pl.ds(g * GROUP, GROUP)
        pltpu.make_async_copy(arrived.at[here], arrived.at[here], recv_sem.at[g]).wait()
        for i in range(GROUP):
            k = g * GROUP + i
            b = codes[0, k] % sensors
            first_re = arrived[k, 0].astype(jnp.float32)
            first_im = arrived[k, 1].astype(jnp.float32)
            second_re = spectra[b, 0].astype(jnp.float32)
            second_im = spectra[b, 1].astype(jnp.float32)
            cross_re = first_re * second_re + first_im * second_im
            cross_im = first_im * second_re - first_re * second_im
            factor = lax.rsqrt(jnp.maximum(cross_re * cross_re + cross_im * cross_im, 1.0))
            rows = pl.ds(i * segments, segments)
            whitened[rows, 0:bins] = (cross_re * factor).astype(jnp.bfloat16)
            whitened[rows, bins:] = (cross_im * factor).astype(jnp.bfloat16)
        summed = jnp.dot(adder, whitened[...], preferred_element_type=jnp.float32)
        high = summed.astype(jnp.bfloat16)
        low = (summed - high.astype(jnp.float32)).astype(jnp.bfloat16)
        both = jnp.dot(jnp.concatenate([high, low], 0), table[...], preferred_element_type=jnp.float32)
        correlation = (both[:GROUP] + both[GROUP:]) * scale
        peaks[here] = jnp.broadcast_to(jnp.max(correlation, axis=-1, keepdims=True), (GROUP, 128))

        @pl.loop(jnp.where(g == 0, 1, 0), GROUP)
        def _(i):
            peak_copy(g * GROUP + i).start()

    own_peak = pltpu.make_async_copy(peaks.at[pl.ds(0, 1)], returned.at[pl.ds(0, 1)], peak_sem)
    own_peak.start()

    def pick(rows, first, values):
        return jnp.sum(jnp.where(rows == lane + first, values, 0.0), axis=0, keepdims=True)

    seconds = [pick(codes_in[...], sensors + first, peaks[...]) for first in range(0, sensors, 128)]
    sent = pl.ds(1, count - 1)
    for buffer, semaphore in ((codes_out, code_send_sem), (outgoing, send_sem), (peaks, peak_send_sem)):
        pltpu.make_async_copy(buffer.at[sent], buffer.at[sent], semaphore).wait()
    pltpu.make_async_copy(returned, returned, peak_sem).wait()
    values = returned[...]
    for i, first in enumerate(range(0, sensors, 128)):
        coherence_out[:, pl.ds(first, 128)] = seconds[i] + pick(own_rows[0], first, values)
    peak_out[...] = pick(own_rows[1], 0, values)


def on_device(spectra, pair_first, pair_second, pair_valid):
    sensors, trailing = spectra.shape[0], spectra.shape[1:]
    count = pair_first.shape[0]
    segments, bins = trailing[1:]
    hbm, smem, vmem = pltpu.HBM, pltpu.SMEM, pltpu.VMEM
    peak, coherence = pl.pallas_call(
        kernel,
        out_shape=(
            vmem((1, count), jnp.float32),
            vmem((1, sensors), jnp.float32),
        ),
        in_specs=[pl.BlockSpec(memory_space=hbm)] * 5,
        out_specs=[pl.BlockSpec(memory_space=vmem)] * 2,
        scratch_shapes=[
            vmem((sensors,) + trailing, jnp.bfloat16),
            vmem((2 * bins, LAGS), jnp.bfloat16),
            vmem((count,) + trailing, jnp.bfloat16),
            vmem((count,) + trailing, jnp.bfloat16),
            vmem((GROUP * segments, 2 * bins), jnp.bfloat16),
            vmem((count, 128), jnp.int32),
            vmem((count, 128), jnp.int32),
            vmem((1, count), jnp.int32),
            smem((1, count), jnp.int32),
            vmem((count, 128), jnp.float32),
            vmem((count, 128), jnp.float32),
            vmem((2, count, 128), jnp.int32),
            smem((count,), jnp.int32),
            smem((count,), jnp.int32),
            smem((count,), jnp.int32),
            smem((count,), jnp.int32),
            smem((count,), jnp.int32),
            pltpu.SemaphoreType.DMA((8,)),
            pltpu.SemaphoreType.DMA,
            pltpu.SemaphoreType.DMA,
            pltpu.SemaphoreType.DMA,
            pltpu.SemaphoreType.DMA((count // GROUP,)),
            pltpu.SemaphoreType.DMA,
            pltpu.SemaphoreType.DMA,
            pltpu.SemaphoreType.DMA,
            pltpu.SemaphoreType.REGULAR,
            pltpu.SemaphoreType.REGULAR,
        ],
        compiler_params=pltpu.CompilerParams(
            collective_id=1, has_side_effects=True, vmem_limit_bytes=60 << 20
        ),
    )(spectra, pair_first, pair_second, pair_valid, lag_table(bins, LAGS))
    return (peak.reshape(-1), coherence.reshape(-1))


def solution(mesh):
    blocks = ("zone", "subzone")
    return jax.shard_map(
        on_device,
        mesh=mesh,
        in_specs=(P(blocks, None, None, None), P(blocks), P(blocks), P(blocks)),
        out_specs=(P(blocks), P(blocks)),
        check_vma=False,
    )
```

```python
import itertools
import math

import jax
import jax.numpy as jnp
import numpy as np
from jax import lax
from jax.experimental import pallas as pl
from jax.experimental.pallas import tpu as pltpu
from jax.sharding import PartitionSpec as P

LAGS = 512
MESH = pl.DeviceIdType.MESH
SIDES = (4, 4, 4, 2)
STRIDES = (32, 8, 2, 1)
GROUP = 8
CODES_AT = 16


def lag_table(bins, lags):
    phase = np.mod(np.arange(bins)[:, None] * (np.arange(lags)[None, :] - lags // 2), 2 * bins)
    phase = phase.astype(np.float64) * (math.pi / bins)
    table = np.concatenate([np.cos(phase), -np.sin(phase)], 0)
    return jnp.asarray(table.astype(np.float32), dtype=jnp.bfloat16)


def orbit(chip):
    found = []
    for turn in range(3):
        turned = chip[turn:] + chip[:turn]
        for way in (turned, tuple(-a % 4 for a in turned)):
            if way not in found:
                found.append(way)
    return found


IN_LINE = [((2, 0, 0), (0, 1))]
IN_PLANE = [((2, 2, 0), (0, 1))]
OTHERS = [
    (chip, (0, 1))
    for chip in (
        (2, 2, 2), (1, 2, 2), (1, 1, 2), (1, 3, 2), (1, 1, 3), (1, 1, 1),
        (1, 2, 0), (2, 1, 0), (1, 3, 0), (1, 1, 0), (1, 0, 0),
    )
]


def spread(parts):
    return [
        way + ((i + core) % 2,) for chip, cores in parts for core in cores for i, way in enumerate(orbit(chip))
    ]


def offsets():
    first = [(0, 0, 0, 0), (0, 0, 0, 1)] + spread(IN_LINE)
    second = first + spread(IN_PLANE)
    order = second + spread(OTHERS)
    assert len(set(order)) == len(order) == 128
    return order, len(first), len(second)


def place(block):
    return (block // 8, block % 8)


def kernel(
    spectra_hbm, first_hbm, second_hbm, valid_hbm, table_hbm, peak_out, coherence_out,
    spectra, table, outgoing, arrived, whitened, codes_out, codes_in, code_row, codes, peaks, returned,
    own_rows, first_ref, second_ref, valid_ref, target, source,
    load_sem, send_sem, code_send_sem, peak_send_sem, recv_sem, code_sem, code_copy_sem, peak_sem, plane_sem, cube_sem,
):
    zone, subzone = lax.axis_index("zone"), lax.axis_index("subzone")
    me = zone * 8 + subzone
    sensors = spectra.shape[0]
    count = arrived.shape[0]
    groups = count // GROUP
    order, lines, planes = offsets()

    loads = [
        pltpu.make_async_copy(a, b, load_sem.at[i])
        for i, (a, b) in enumerate(
            [(first_hbm, first_ref), (second_hbm, second_ref), (valid_hbm, valid_ref), (table_hbm, table)]
        )
    ]
    share = sensors // 4
    parts = tuple(
        pltpu.make_async_copy(spectra_hbm.at[pl.ds(i * share, share)], spectra.at[pl.ds(i * share, share)], load_sem.at[4 + i])
        for i in range(4)
    )
    for load in (loads[0],) + parts + tuple(loads[1:]):
        load.start()

    here = (zone // 4, zone % 4, subzone // 2, subzone % 2)
    ahead = [[(h + o) % n * s for o in range(n)] for h, n, s in zip(here, SIDES, STRIDES)]

    def signal(semaphore, ways):
        for way in ways:
            other = sum(ahead[a][o] for a, o in enumerate(way))
            pl.semaphore_signal(semaphore, inc=1, device_id=place(other), device_id_type=MESH)

    along_y = [(i, 0, 0, 0) for i in (1, 3, 2)]
    along_x = [(0, i, 0, 0) for i in (1, 3, 2)]
    barrier = pltpu.get_barrier_semaphore()
    in_line = [
        way[:3] + (core,) for i in (2, 1, 3) for way in ((i, 0, 0), (0, i, 0), (0, 0, i)) for core in range(2)
    ] + [(0, 0, 0, 1)]
    signal(barrier, in_line)

    def locate(low, high):
        for k in range(low, high):
            target[k] = sum(ahead[a][o] for a, o in enumerate(order[k]))

    pl.semaphore_wait(barrier, len(in_line))
    signal(plane_sem, along_x + along_y)
    locate(0, planes)
    for load in (loads[0],) + parts:
        load.wait()

    def code_copy(k):
        return pltpu.make_async_remote_copy(
            src_ref=codes_out.at[pl.ds(k, 1)],
            dst_ref=codes_in.at[pl.ds(k, 1)],
            send_sem=code_send_sem,
            recv_sem=code_sem,
            device_id=place(target[k]),
            device_id_type=MESH,
        )

    def spectrum_copy(k):
        return pltpu.make_async_remote_copy(
            src_ref=outgoing.at[k],
            dst_ref=arrived.at[k],
            send_sem=send_sem,
            recv_sem=recv_sem.at[k // GROUP],
            device_id=place(target[k]),
            device_id_type=MESH,
        )

    def peak_copy(k):
        return pltpu.make_async_remote_copy(
            src_ref=peaks.at[pl.ds(k, 1)],
            dst_ref=returned.at[pl.ds(k, 1)],
            send_sem=peak_send_sem,
            recv_sem=peak_sem,
            device_id=place(source[k]),
            device_id_type=MESH,
        )

    def pack(k):
        outgoing[k] = spectra[first_ref[target[k]] % sensors]

    def send(low, high):
        @pl.loop(low, high)
        def _(k):
            pack(k)
            spectrum_copy(k).start()

    send(1, lines)
    pl.semaphore_wait(plane_sem, 6)
    signal(cube_sem, along_x)
    send(lines, planes)
    locate(planes, count)
    pl.semaphore_wait(cube_sem, 3)
    send(planes, CODES_AT)
    for load in loads[1:3]:
        load.wait()
    for k, offset in enumerate(order):
        source[k] = sum(ahead[a][-o % SIDES[a]] for a, o in enumerate(offset))

    @pl.loop(0, count)
    def _(k):
        pair = target[k]
        in_use = valid_ref[pair]
        row = pl.ds(k, 1)
        codes_out[row] = jnp.full((1, 128), second_ref[pair] % sensors + in_use * sensors, jnp.int32)

        @pl.when(k > 0)
        def _():
            code_copy(k).start()

    pack(0)
    own_spectrum = pltpu.make_async_copy(outgoing.at[0], arrived.at[0], recv_sem.at[0])
    own_spectrum.start()
    own_code = pltpu.make_async_copy(codes_out.at[pl.ds(0, 1)], codes_in.at[pl.ds(0, 1)], code_sem)
    own_code.start()
    send(CODES_AT, count)

    @pl.loop(0, count)
    def _(k):
        pair = target[k]
        in_use = valid_ref[pair]
        row = pl.ds(k, 1)
        own_rows[0, row] = jnp.full((1, 128), first_ref[pair] % sensors + (1 - in_use) * sensors, jnp.int32)
        own_rows[1, row] = jnp.full((1, 128), pair + (1 - in_use) * sensors, jnp.int32)

    pltpu.make_async_copy(codes_in, codes_in, code_sem).wait()
    lane = lax.broadcasted_iota(jnp.int32, (count, 128), 1)
    slot = lax.broadcasted_iota(jnp.int32, (count, 128), 0)
    code_row[...] = jnp.sum(jnp.where(lane == slot, codes_in[...], 0), axis=0, keepdims=True)
    copy = pltpu.make_async_copy(code_row, codes, code_copy_sem)
    copy.start()
    copy.wait()
    loads[3].wait()

    segments, bins = spectra.shape[2:]
    depth = GROUP * segments
    row_of = lax.broadcasted_iota(jnp.int32, (GROUP, depth), 0)
    segment_of = lax.broadcasted_iota(jnp.int32, (GROUP, depth), 1)
    adder = jnp.where(segment_of // segments == row_of, 1.0, 0.0).astype(jnp.bfloat16)
    scale = bins ** (-0.5) / segments

    @pl.loop(0, groups)
    def _(g):
        here = pl.ds(g * GROUP, GROUP)
        pltpu.make_async_copy(arrived.at[here], arrived.at[here], recv_sem.at[g]).wait()
        for i in range(GROUP):
            k = g * GROUP + i
            b = codes[0, k] % sensors
            first_re = arrived[k, 0].astype(jnp.float32)
            first_im = arrived[k, 1].astype(jnp.float32)
            second_re = spectra[b, 0].astype(jnp.float32)
            second_im = spectra[b, 1].astype(jnp.float32)
            cross_re = first_re * second_re + first_im * second_im
            cross_im = first_im * second_re - first_re * second_im
            factor = lax.rsqrt(jnp.maximum(cross_re * cross_re + cross_im * cross_im, 1.0))
            rows = pl.ds(i * segments, segments)
            whitened[rows, 0:bins] = (cross_re * factor).astype(jnp.bfloat16)
            whitened[rows, bins:] = (cross_im * factor).astype(jnp.bfloat16)
        summed = jnp.dot(adder, whitened[...], preferred_element_type=jnp.float32)
        high = summed.astype(jnp.bfloat16)
        low = (summed - high.astype(jnp.float32)).astype(jnp.bfloat16)
        both = jnp.dot(jnp.concatenate([high, low], 0), table[...], preferred_element_type=jnp.float32)
        correlation = (both[:GROUP] + both[GROUP:]) * scale
        peaks[here] = jnp.broadcast_to(jnp.max(correlation, axis=-1, keepdims=True), (GROUP, 128))

        @pl.loop(jnp.where(g == 0, 1, 0), GROUP)
        def _(i):
            peak_copy(g * GROUP + i).start()

    own_peak = pltpu.make_async_copy(peaks.at[pl.ds(0, 1)], returned.at[pl.ds(0, 1)], peak_sem)
    own_peak.start()

    def pick(rows, first, values):
        return jnp.sum(jnp.where(rows == lane + first, values, 0.0), axis=0, keepdims=True)

    seconds = [pick(codes_in[...], sensors + first, peaks[...]) for first in range(0, sensors, 128)]
    sent = pl.ds(1, count - 1)
    for buffer, semaphore in ((codes_out, code_send_sem), (outgoing, send_sem), (peaks, peak_send_sem)):
        pltpu.make_async_copy(buffer.at[sent], buffer.at[sent], semaphore).wait()
    pltpu.make_async_copy(returned, returned, peak_sem).wait()
    values = returned[...]
    for i, first in enumerate(range(0, sensors, 128)):
        coherence_out[:, pl.ds(first, 128)] = seconds[i] + pick(own_rows[0], first, values)
    peak_out[...] = pick(own_rows[1], 0, values)


def on_device(spectra, pair_first, pair_second, pair_valid):
    sensors, trailing = spectra.shape[0], spectra.shape[1:]
    count = pair_first.shape[0]
    segments, bins = trailing[1:]
    hbm, smem, vmem = pltpu.HBM, pltpu.SMEM, pltpu.VMEM
    peak, coherence = pl.pallas_call(
        kernel,
        out_shape=(
            vmem((1, count), jnp.float32),
            vmem((1, sensors), jnp.float32),
        ),
        in_specs=[pl.BlockSpec(memory_space=hbm)] * 5,
        out_specs=[pl.BlockSpec(memory_space=vmem)] * 2,
        scratch_shapes=[
            vmem((sensors,) + trailing, jnp.bfloat16),
            vmem((2 * bins, LAGS), jnp.bfloat16),
            vmem((count,) + trailing, jnp.bfloat16),
            vmem((count,) + trailing, jnp.bfloat16),
            vmem((GROUP * segments, 2 * bins), jnp.bfloat16),
            vmem((count, 128), jnp.int32),
            vmem((count, 128), jnp.int32),
            vmem((1, count), jnp.int32),
            smem((1, count), jnp.int32),
            vmem((count, 128), jnp.float32),
            vmem((count, 128), jnp.float32),
            vmem((2, count, 128), jnp.int32),
            smem((count,), jnp.int32),
            smem((count,), jnp.int32),
            smem((count,), jnp.int32),
            smem((count,), jnp.int32),
            smem((count,), jnp.int32),
            pltpu.SemaphoreType.DMA((8,)),
            pltpu.SemaphoreType.DMA,
            pltpu.SemaphoreType.DMA,
            pltpu.SemaphoreType.DMA,
            pltpu.SemaphoreType.DMA((count // GROUP,)),
            pltpu.SemaphoreType.DMA,
            pltpu.SemaphoreType.DMA,
            pltpu.SemaphoreType.DMA,
            pltpu.SemaphoreType.REGULAR,
            pltpu.SemaphoreType.REGULAR,
        ],
        compiler_params=pltpu.CompilerParams(
            collective_id=1, has_side_effects=True, vmem_limit_bytes=60 << 20
        ),
    )(spectra, pair_first, pair_second, pair_valid, lag_table(bins, LAGS))
    return (peak.reshape(-1), coherence.reshape(-1))


def solution(mesh):
    blocks = ("zone", "subzone")
    return jax.shard_map(
        on_device,
        mesh=mesh,
        in_specs=(P(blocks, None, None, None), P(blocks), P(blocks), P(blocks)),
        out_specs=(P(blocks), P(blocks)),
        check_vma=False,
    )
```

```python
import itertools
import math

import jax
import jax.numpy as jnp
import numpy as np
from jax import lax
from jax.experimental import pallas as pl
from jax.experimental.pallas import tpu as pltpu
from jax.sharding import PartitionSpec as P

LAGS = 512
MESH = pl.DeviceIdType.MESH
SIDES = (4, 4, 4, 2)
STRIDES = (32, 8, 2, 1)
GROUP = 8
CODES_AT = 16


def lag_table(bins, lags):
    phase = np.mod(np.arange(bins)[:, None] * (np.arange(lags)[None, :] - lags // 2), 2 * bins)
    phase = phase.astype(np.float64) * (math.pi / bins)
    table = np.concatenate([np.cos(phase), -np.sin(phase)], 0)
    return jnp.asarray(table.astype(np.float32), dtype=jnp.bfloat16)


def orbit(chip):
    found = []
    for turn in range(3):
        turned = chip[turn:] + chip[:turn]
        for way in (turned, tuple(-a % 4 for a in turned)):
            if way not in found:
                found.append(way)
    return found


IN_LINE = [((2, 0, 0), (0, 1))]
IN_PLANE = [((2, 2, 0), (0, 1))]
OTHERS = [
    (chip, (0, 1))
    for chip in (
        (1, 1, 1), (1, 1, 3), (1, 3, 2), (1, 1, 2), (1, 2, 2), (2, 2, 2),
        (1, 2, 0), (2, 1, 0), (1, 3, 0), (1, 1, 0), (1, 0, 0),
    )
]


def spread(parts):
    return [
        way + ((i + core) % 2,) for chip, cores in parts for core in cores for i, way in enumerate(orbit(chip))
    ]


def offsets():
    first = [(0, 0, 0, 0), (0, 0, 0, 1)] + spread(IN_LINE)
    second = first + spread(IN_PLANE)
    order = second + spread(OTHERS)
    assert len(set(order)) == len(order) == 128
    return order, len(first), len(second)


def place(block):
    return (block // 8, block % 8)


def kernel(
    spectra_hbm, first_hbm, second_hbm, valid_hbm, table_hbm, peak_out, coherence_out,
    spectra, table, outgoing, arrived, whitened, codes_out, codes_in, code_row, codes, peaks, returned,
    own_rows, first_ref, second_ref, valid_ref, target, source,
    load_sem, send_sem, code_send_sem, peak_send_sem, recv_sem, code_sem, code_copy_sem, peak_sem, plane_sem, cube_sem,
):
    zone, subzone = lax.axis_index("zone"), lax.axis_index("subzone")
    me = zone * 8 + subzone
    sensors = spectra.shape[0]
    count = arrived.shape[0]
    groups = count // GROUP
    order, lines, planes = offsets()

    loads = [
        pltpu.make_async_copy(a, b, load_sem.at[i])
        for i, (a, b) in enumerate(
            [(first_hbm, first_ref), (second_hbm, second_ref), (valid_hbm, valid_ref), (table_hbm, table)]
        )
    ]
    share = sensors // 4
    parts = tuple(
        pltpu.make_async_copy(spectra_hbm.at[pl.ds(i * share, share)], spectra.at[pl.ds(i * share, share)], load_sem.at[4 + i])
        for i in range(4)
    )
    for load in (loads[0],) + parts + tuple(loads[1:]):
        load.start()

    here = (zone // 4, zone % 4, subzone // 2, subzone % 2)
    ahead = [[(h + o) % n * s for o in range(n)] for h, n, s in zip(here, SIDES, STRIDES)]

    def signal(semaphore, ways):
        for way in ways:
            other = sum(ahead[a][o] for a, o in enumerate(way))
            pl.semaphore_signal(semaphore, inc=1, device_id=place(other), device_id_type=MESH)

    along_y = [(i, 0, 0, 0) for i in (1, 3, 2)]
    along_x = [(0, i, 0, 0) for i in (1, 3, 2)]
    barrier = pltpu.get_barrier_semaphore()
    in_line = [
        way[:3] + (core,) for i in (2, 1, 3) for way in ((i, 0, 0), (0, i, 0), (0, 0, i)) for core in range(2)
    ] + [(0, 0, 0, 1)]
    signal(barrier, in_line)

    def locate(low, high):
        for k in range(low, high):
            target[k] = sum(ahead[a][o] for a, o in enumerate(order[k]))

    pl.semaphore_wait(barrier, len(in_line))
    signal(plane_sem, along_x + along_y)
    locate(0, planes)
    for load in (loads[0],) + parts:
        load.wait()

    def code_copy(k):
        return pltpu.make_async_remote_copy(
            src_ref=codes_out.at[pl.ds(k, 1)],
            dst_ref=codes_in.at[pl.ds(k, 1)],
            send_sem=code_send_sem,
            recv_sem=code_sem,
            device_id=place(target[k]),
            device_id_type=MESH,
        )

    def spectrum_copy(k):
        return pltpu.make_async_remote_copy(
            src_ref=outgoing.at[k],
            dst_ref=arrived.at[k],
            send_sem=send_sem,
            recv_sem=recv_sem.at[k // GROUP],
            device_id=place(target[k]),
            device_id_type=MESH,
        )

    def peak_copy(k):
        return pltpu.make_async_remote_copy(
            src_ref=peaks.at[pl.ds(k, 1)],
            dst_ref=returned.at[pl.ds(k, 1)],
            send_sem=peak_send_sem,
            recv_sem=peak_sem,
            device_id=place(source[k]),
            device_id_type=MESH,
        )

    def pack(k):
        outgoing[k] = spectra[first_ref[target[k]] % sensors]

    def send(low, high):
        @pl.loop(low, high)
        def _(k):
            pack(k)
            spectrum_copy(k).start()

    send(1, lines)
    pl.semaphore_wait(plane_sem, 6)
    signal(cube_sem, along_x)
    send(lines, planes)
    locate(planes, count)
    pl.semaphore_wait(cube_sem, 3)
    send(planes, CODES_AT)
    for load in loads[1:3]:
        load.wait()
    for k, offset in enumerate(order):
        source[k] = sum(ahead[a][-o % SIDES[a]] for a, o in enumerate(offset))

    @pl.loop(0, count)
    def _(k):
        pair = target[k]
        in_use = valid_ref[pair]
        row = pl.ds(k, 1)
        codes_out[row] = jnp.full((1, 128), second_ref[pair] % sensors + in_use * sensors, jnp.int32)

        @pl.when(k > 0)
        def _():
            code_copy(k).start()

    pack(0)
    own_spectrum = pltpu.make_async_copy(outgoing.at[0], arrived.at[0], recv_sem.at[0])
    own_spectrum.start()
    own_code = pltpu.make_async_copy(codes_out.at[pl.ds(0, 1)], codes_in.at[pl.ds(0, 1)], code_sem)
    own_code.start()
    send(CODES_AT, count)

    @pl.loop(0, count)
    def _(k):
        pair = target[k]
        in_use = valid_ref[pair]
        row = pl.ds(k, 1)
        own_rows[0, row] = jnp.full((1, 128), first_ref[pair] % sensors + (1 - in_use) * sensors, jnp.int32)
        own_rows[1, row] = jnp.full((1, 128), pair + (1 - in_use) * sensors, jnp.int32)

    pltpu.make_async_copy(codes_in, codes_in, code_sem).wait()
    lane = lax.broadcasted_iota(jnp.int32, (count, 128), 1)
    slot = lax.broadcasted_iota(jnp.int32, (count, 128), 0)
    code_row[...] = jnp.sum(jnp.where(lane == slot, codes_in[...], 0), axis=0, keepdims=True)
    copy = pltpu.make_async_copy(code_row, codes, code_copy_sem)
    copy.start()
    copy.wait()
    loads[3].wait()

    segments, bins = spectra.shape[2:]
    depth = GROUP * segments
    row_of = lax.broadcasted_iota(jnp.int32, (GROUP, depth), 0)
    segment_of = lax.broadcasted_iota(jnp.int32, (GROUP, depth), 1)
    adder = jnp.where(segment_of // segments == row_of, 1.0, 0.0).astype(jnp.bfloat16)
    scale = bins ** (-0.5) / segments

    @pl.loop(0, groups)
    def _(g):
        here = pl.ds(g * GROUP, GROUP)
        pltpu.make_async_copy(arrived.at[here], arrived.at[here], recv_sem.at[g]).wait()
        for i in range(GROUP):
            k = g * GROUP + i
            b = codes[0, k] % sensors
            first_re = arrived[k, 0].astype(jnp.float32)
            first_im = arrived[k, 1].astype(jnp.float32)
            second_re = spectra[b, 0].astype(jnp.float32)
            second_im = spectra[b, 1].astype(jnp.float32)
            cross_re = first_re * second_re + first_im * second_im
            cross_im = first_im * second_re - first_re * second_im
            factor = lax.rsqrt(jnp.maximum(cross_re * cross_re + cross_im * cross_im, 1.0))
            rows = pl.ds(i * segments, segments)
            whitened[rows, 0:bins] = (cross_re * factor).astype(jnp.bfloat16)
            whitened[rows, bins:] = (cross_im * factor).astype(jnp.bfloat16)
        summed = jnp.dot(adder, whitened[...], preferred_element_type=jnp.float32)
        high = summed.astype(jnp.bfloat16)
        low = (summed - high.astype(jnp.float32)).astype(jnp.bfloat16)
        both = jnp.dot(jnp.concatenate([high, low], 0), table[...], preferred_element_type=jnp.float32)
        correlation = (both[:GROUP] + both[GROUP:]) * scale
        peaks[here] = jnp.broadcast_to(jnp.max(correlation, axis=-1, keepdims=True), (GROUP, 128))

        @pl.loop(jnp.where(g == 0, 1, 0), GROUP)
        def _(i):
            peak_copy(g * GROUP + i).start()

    own_peak = pltpu.make_async_copy(peaks.at[pl.ds(0, 1)], returned.at[pl.ds(0, 1)], peak_sem)
    own_peak.start()

    def pick(rows, first, values):
        return jnp.sum(jnp.where(rows == lane + first, values, 0.0), axis=0, keepdims=True)

    seconds = [pick(codes_in[...], sensors + first, peaks[...]) for first in range(0, sensors, 128)]
    sent = pl.ds(1, count - 1)
    for buffer, semaphore in ((codes_out, code_send_sem), (outgoing, send_sem), (peaks, peak_send_sem)):
        pltpu.make_async_copy(buffer.at[sent], buffer.at[sent], semaphore).wait()
    pltpu.make_async_copy(returned, returned, peak_sem).wait()
    values = returned[...]
    for i, first in enumerate(range(0, sensors, 128)):
        coherence_out[:, pl.ds(first, 128)] = seconds[i] + pick(own_rows[0], first, values)
    peak_out[...] = pick(own_rows[1], 0, values)


def on_device(spectra, pair_first, pair_second, pair_valid):
    sensors, trailing = spectra.shape[0], spectra.shape[1:]
    count = pair_first.shape[0]
    segments, bins = trailing[1:]
    hbm, smem, vmem = pltpu.HBM, pltpu.SMEM, pltpu.VMEM
    peak, coherence = pl.pallas_call(
        kernel,
        out_shape=(
            vmem((1, count), jnp.float32),
            vmem((1, sensors), jnp.float32),
        ),
        in_specs=[pl.BlockSpec(memory_space=hbm)] * 5,
        out_specs=[pl.BlockSpec(memory_space=vmem)] * 2,
        scratch_shapes=[
            vmem((sensors,) + trailing, jnp.bfloat16),
            vmem((2 * bins, LAGS), jnp.bfloat16),
            vmem((count,) + trailing, jnp.bfloat16),
            vmem((count,) + trailing, jnp.bfloat16),
            vmem((GROUP * segments, 2 * bins), jnp.bfloat16),
            vmem((count, 128), jnp.int32),
            vmem((count, 128), jnp.int32),
            vmem((1, count), jnp.int32),
            smem((1, count), jnp.int32),
            vmem((count, 128), jnp.float32),
            vmem((count, 128), jnp.float32),
            vmem((2, count, 128), jnp.int32),
            smem((count,), jnp.int32),
            smem((count,), jnp.int32),
            smem((count,), jnp.int32),
            smem((count,), jnp.int32),
            smem((count,), jnp.int32),
            pltpu.SemaphoreType.DMA((8,)),
            pltpu.SemaphoreType.DMA,
            pltpu.SemaphoreType.DMA,
            pltpu.SemaphoreType.DMA,
            pltpu.SemaphoreType.DMA((count // GROUP,)),
            pltpu.SemaphoreType.DMA,
            pltpu.SemaphoreType.DMA,
            pltpu.SemaphoreType.DMA,
            pltpu.SemaphoreType.REGULAR,
            pltpu.SemaphoreType.REGULAR,
        ],
        compiler_params=pltpu.CompilerParams(
            collective_id=1, has_side_effects=True, vmem_limit_bytes=60 << 20
        ),
    )(spectra, pair_first, pair_second, pair_valid, lag_table(bins, LAGS))
    return (peak.reshape(-1), coherence.reshape(-1))


def solution(mesh):
    blocks = ("zone", "subzone")
    return jax.shard_map(
        on_device,
        mesh=mesh,
        in_specs=(P(blocks, None, None, None), P(blocks), P(blocks), P(blocks)),
        out_specs=(P(blocks), P(blocks)),
        check_vma=False,
    )
```
